32 devices in a mesh: sub: 2 (over y), row: 8 (over z, x), col: 2 (over core).
Axes of the slice: x: 2, y: 2, z: 4, core: 2. Of those that a mesh axis runs over, the one named last changes fastest.
Arguments:
- child_pivot: float32 [2, 1024, 1024], P('sub', 'row'), as said below
- child_border: float32 [2, 4096, 1024], P('sub', 'row'), as said below
- child_update: float32 [2, 4096, 4096], P('sub', 'row', 'col'), as said below
- parent_front: float32 [16384, 16384], P('row', ('sub', 'col')), as said below
- tile_map: int32 [2, 32], replicated, may hold values from -1 to 127, as said below
Outputs:
- schur_block: float32 [16384, 16384], P('row', ('sub', 'col'))
- panel_rows: float32 [16384, 256], P('row')
The draws below stay inside these ranges and needn't reach their ends.
Inputs may be any that keep to these rules, and one draw needn't show every extreme that they name: For each child s the matrix [[child_pivot[s], child_border[s]^T], [child_border[s], child_update[s]]] is symmetric positive definite; child_pivot[s] and child_update[s] are symmetric. `child_border`: see child_pivot: the border of a symmetric positive definite child front. `child_update`: see child_pivot: the trailing block of a symmetric positive definite child front. `parent_front`: symmetric positive definite. tile_map[s, t] is the parent tile that receives tile t of child s, or -1 where t lies beyond child s's front; the -1 entries of a child come after its live ones, every child has 16 live tiles or more, some child has all 32 live and some exactly 16; the live entries of one child are distinct; the child tiles t with t // 4 == i map into parent tiles i * 16 to (i + 1) * 16 - 1.
All inputs are finite; a program needn't handle non-finite values.
Results may differ from the reference program's by a relative error of at most 0.0001.
Values sent between devices are 32-bit elements; how exact they have to be, the bound alone decides.
A program may use at most 192 MiB of HBM per device.

```python
import math
import jax
import jax.numpy as jnp
from jax import lax

PIVOTS = 1024
CONTRIB = 4096
PARENT = 16384
PANEL = 256
TILE = 128
CHILDREN = 2
CTILES = 32
CT_ROW = 4
PT_ROW = 16


def entries(key, shape, sigma):
    values = jax.random.normal(key, shape, jnp.float32)
    return values * sigma


def child_sigma():
    return 1.5 / math.sqrt(PIVOTS + CONTRIB)


def symmetric_blocks(key, salt, count, sigma, low, high):
    raw = entries(jax.random.fold_in(key, salt), (CHILDREN, count, count), sigma)
    mirrored = (raw + jnp.swapaxes(raw, 1, 2)) * 0.70710678
    diagonal = jax.random.uniform(jax.random.fold_in(key, salt + 1), (CHILDREN, count), jnp.float32, low, high)
    unit = jnp.eye(count, dtype=jnp.float32)
    return mirrored * (1.0 - unit) + diagonal[:, :, None] * unit


def draw_child_pivot(key, part):
    block = symmetric_blocks(key, 21, PIVOTS, child_sigma(), 4.5, 6.0)
    return block


def draw_child_border(key, part):
    raw = entries(jax.random.fold_in(key, 23), (CHILDREN, CONTRIB, PIVOTS), child_sigma())
    return raw


def draw_child_update(key, part):
    block = symmetric_blocks(key, 25, CONTRIB, child_sigma(), 4.5, 6.0)
    return block


def draw_parent_front(key, part):
    raw = entries(jax.random.fold_in(key, 41), (PARENT, PARENT), 1.0 / math.sqrt(PARENT))
    mirrored = (raw + raw.T) * 0.70710678
    diagonal = jax.random.uniform(jax.random.fold_in(key, 42), (PARENT,), jnp.float32, 2.5, 3.5)
    unit = jnp.eye(PARENT, dtype=jnp.float32)
    block = mirrored * (1.0 - unit) + diagonal[:, None] * unit
    return block


def draw_tile_map(key, part):
    block_count = CTILES // CT_ROW
    total_blocks = CHILDREN * block_count
    perm_keys = jax.random.split(jax.random.fold_in(key, 5), total_blocks)
    ranked = jax.vmap(lambda subkey: jax.random.permutation(subkey, PT_ROW))(perm_keys)[:, :CT_ROW]
    lower_keys = jax.random.split(jax.random.fold_in(key, 8), total_blocks)
    lower_ranked = jax.vmap(lambda subkey: jax.random.permutation(subkey, PT_ROW - 1))(lower_keys)[:, :CT_ROW - 1]
    with_last = jnp.concatenate([lower_ranked.astype(jnp.int32), jnp.full((total_blocks, 1), PT_ROW - 1, jnp.int32)], axis=1)
    order_keys = jax.random.split(jax.random.fold_in(key, 9), total_blocks)
    orders = jax.vmap(lambda subkey: jax.random.permutation(subkey, CT_ROW))(order_keys).astype(jnp.int32)
    forced = jnp.take_along_axis(with_last, orders, axis=1)
    shuffle = jax.random.permutation(jax.random.fold_in(key, 7), CHILDREN)
    child_ids = jnp.arange(CHILDREN, dtype=jnp.int32)[:, None] * jnp.ones((1, block_count), jnp.int32)
    block_ids = jnp.ones((CHILDREN, 1), jnp.int32) * jnp.arange(block_count, dtype=jnp.int32)[None, :]
    target = ((child_ids == shuffle[0]) & (block_ids == block_count - 1)).reshape(total_blocks)
    picked = jnp.where(target[:, None], forced, ranked.astype(jnp.int32))
    block_start = jnp.arange(block_count, dtype=jnp.int32) * PT_ROW
    chosen = picked.reshape(CHILDREN, block_count, CT_ROW) + block_start[None, :, None]
    chosen = chosen.reshape(CHILDREN, CTILES)
    live_count = jax.random.randint(jax.random.fold_in(key, 6), (CHILDREN,), CTILES // 2, CTILES + 1)
    live_count = live_count.at[shuffle[0]].set(CTILES).at[shuffle[1]].set(CTILES // 2)
    positions = jnp.arange(CTILES, dtype=jnp.int32)
    return jnp.where(positions[None, :] < live_count[:, None], chosen, -1).astype(jnp.int32)


def setup_inputs(seed: int = 0) -> dict:
    splits = jax.random.split(jax.random.key(seed), 6)
    child_pivot = draw_child_pivot(jax.random.fold_in(splits[5], 71), 0)
    child_border = draw_child_border(jax.random.fold_in(splits[5], 71), 0)
    child_update = draw_child_update(jax.random.fold_in(splits[5], 71), 0)
    parent_front = draw_parent_front(jax.random.fold_in(splits[5], 71), 0)
    tile_map = draw_tile_map(jax.random.fold_in(splits[5], 71), 0)
    return dict(child_pivot=child_pivot, child_border=child_border, child_update=child_update, parent_front=parent_front, tile_map=tile_map)


highest = lax.Precision.HIGHEST

def solve_rows(lower_tri, right_rows):
    return jax.scipy.linalg.solve_triangular(lower_tri, right_rows.T, lower=True).T

def contribution(pivot_block, border, update):
    lower_tri = jnp.linalg.cholesky(pivot_block)
    factor = solve_rows(lower_tri, border)
    return update - jnp.dot(factor.astype(jnp.float32), factor.T.astype(jnp.float32), precision=highest, preferred_element_type=jnp.float32)

def reference(child_pivot, child_border, child_update, parent_front, tile_map):
    offsets = jnp.arange(TILE, dtype=jnp.int32)
    parent = parent_front
    for member in range(CHILDREN):
        contrib = contribution(child_pivot[member], child_border[member], child_update[member])
        tile_ids = tile_map[member].astype(jnp.int32)
        indices = (tile_ids[:, None] * TILE + offsets[None, :]).reshape(-1)
        indices = jnp.where(indices >= 0, indices, PARENT).astype(jnp.int32)
        parent = parent.at[indices[:, None], indices[None, :]].add(contrib, mode='drop')
    top_lower = jnp.linalg.cholesky(parent[:PANEL, :PANEL])
    panel_rows = solve_rows(top_lower, parent[:, :PANEL])
    schur_block = parent - jnp.dot(panel_rows.astype(jnp.float32), panel_rows.T.astype(jnp.float32), precision=highest, preferred_element_type=jnp.float32)
    return (schur_block, panel_rows)
```

```python
import functools

import jax
import jax.numpy as jnp
from jax import lax
from jax.experimental import pallas as pl
from jax.experimental.pallas import tpu as pltpu
from jax.sharding import PartitionSpec as P

PANEL = 256
TILE = 128
STRIP = 32
SLAB = 256

high = lax.Precision.HIGH
highest = lax.Precision.HIGHEST
BY_COLUMNS = (((1,), (1,)), ((), ()))


def mm(left, right):
    return jnp.dot(left, right, precision=highest, preferred_element_type=jnp.float32)


def times_transposed(left, right):
    return lax.dot_general(
        left, right, BY_COLUMNS, precision=high, preferred_element_type=jnp.float32
    )


def invert_tile(block):
    lane = lax.broadcasted_iota(jnp.int32, (STRIP, TILE), 1)
    row = lax.broadcasted_iota(jnp.int32, (STRIP, TILE), 0)
    first = 0
    rest = block
    done = []
    while first < TILE:
        strip = rest[:STRIP]
        for step in range(STRIP):
            pivot = first + step
            scale = lax.rsqrt(strip[step : step + 1, pivot : pivot + 1])
            column = jnp.broadcast_to(strip[:, pivot : pivot + 1], (STRIP, TILE))
            at_pivot = lane == pivot
            scaled = jnp.where(at_pivot[:1], 1.0, strip[step : step + 1]) * scale
            below = jnp.where(row > step, column, 0.0) * scale
            kept = jnp.where(at_pivot, 0.0, strip) - below * scaled
            strip = jnp.where(row == step, jnp.broadcast_to(scaled, (STRIP, TILE)), kept)
        done.append(strip)
        first += STRIP
        if first < TILE:
            rest = rest[STRIP:]
            columns = lax.broadcasted_iota(jnp.int32, rest.shape, 1)
            cleared = (columns >= first - STRIP) & (columns < first)
            rest = jnp.where(cleared, 0.0, rest) - mm(strip.T[first:], strip)
    whole = jnp.concatenate(done, axis=0)
    lane = lax.broadcasted_iota(jnp.int32, (TILE, TILE), 1)
    row = lax.broadcasted_iota(jnp.int32, (TILE, TILE), 0)
    return jnp.where(lane > row, 0.0, whole)


def invert_factor(work, strip):
    order = work.shape[0]
    tiles = order // TILE

    def tile_at(index):
        return pl.ds(pl.multiple_of(index * TILE, TILE), TILE)

    def eliminate(k, carry):
        here = tile_at(k)
        corner = invert_tile(work[here, here])
        strip[...] = mm(corner, work[here, :])
        strip[:, here] = corner

        def update(i, inner):
            there = tile_at(i)
            work[there, here] = jnp.zeros((TILE, TILE), jnp.float32)
            work[there, :] = work[there, :] - mm(strip[:, there].T, strip[...])
            return inner

        lax.fori_loop(k + 1, tiles, update, 0)
        columns = lax.broadcasted_iota(jnp.int32, (TILE, order), 1)
        work[here, :] = jnp.where(columns < (k + 1) * TILE, strip[...], 0.0)
        return carry

    lax.fori_loop(0, tiles, eliminate, 0)


def pivot_kernel(pivot_ref, inverse_ref, strip):
    inverse_ref[...] = pivot_ref[...]
    invert_factor(inverse_ref, strip)


def whole_block(shape):
    return pl.BlockSpec(shape, lambda *_: (0,) * len(shape))


def invert_pivot(pivot):
    order = pivot.shape[0]
    return pl.pallas_call(
        pivot_kernel,
        out_shape=jax.ShapeDtypeStruct((order, order), jnp.float32),
        in_specs=[pl.BlockSpec(memory_space=pltpu.VMEM)],
        out_specs=pl.BlockSpec(memory_space=pltpu.VMEM),
        scratch_shapes=[pltpu.VMEM((TILE, order), jnp.float32)],
        compiler_params=pltpu.CompilerParams(vmem_limit_bytes=40 * 2**20),
        cost_estimate=pl.CostEstimate(
            flops=40 * order**3, bytes_accessed=8 * order**2, transcendentals=order
        ),
        name="invert_pivot",
    )(pivot)


def add_row_tiles(map_ref, first, tiles, limit, sent_ref, target):
    for child in range(sent_ref.shape[0]):
        for r in range(tiles):
            place = map_ref[child, first + r]

            @pl.when((place >= 0) & (lax.rem(jnp.maximum(place, 0), limit[0]) < limit[1]))
            def _():
                spot = lax.rem(place, limit[0])
                rows = pl.ds(pl.multiple_of(spot * TILE, TILE), TILE)
                target[rows, :] += sent_ref[child, r * TILE : (r + 1) * TILE, :]


def top_kernel(block_tiles, map_ref, front_ref, sent_ref, inverse_ref, strip):
    inverse_ref[...] = front_ref[...]
    tiles = sent_ref.shape[1] // TILE
    add_row_tiles(map_ref, 0, tiles, (block_tiles, PANEL // TILE), sent_ref, inverse_ref)
    invert_factor(inverse_ref, strip)


def invert_top(tile_map, front_panel, sent, block_rows, child_rows):
    children = sent.shape[0]
    return pl.pallas_call(
        functools.partial(top_kernel, block_rows // TILE),
        out_shape=jax.ShapeDtypeStruct((PANEL, PANEL), jnp.float32),
        grid_spec=pltpu.PrefetchScalarGridSpec(
            num_scalar_prefetch=1,
            grid=(1,),
            in_specs=[
                whole_block((PANEL, PANEL)),
                whole_block((children, child_rows, PANEL)),
            ],
            out_specs=whole_block((PANEL, PANEL)),
            scratch_shapes=[pltpu.VMEM((TILE, PANEL), jnp.float32)],
        ),
        compiler_params=pltpu.CompilerParams(vmem_limit_bytes=32 * 2**20),
        name="invert_top",
    )(tile_map, front_panel, sent)


def panel_kernel(block_tiles, ids_ref, map_ref, front_ref, sent_ref, inverse_ref, out_ref, held):
    held[...] = front_ref[...]
    tiles = sent_ref.shape[1] // TILE
    first = ids_ref[pl.program_id(0)] * tiles
    add_row_tiles(map_ref, first, tiles, (block_tiles, block_tiles), sent_ref, held)
    out_ref[...] = lax.dot_general(
        held[...], inverse_ref[...], BY_COLUMNS, precision=highest,
        preferred_element_type=jnp.float32,
    )


def factor_panel(block_ids, tile_map, front_panel, sent, inverse, block_rows, child_rows):
    children = sent.shape[0]
    count = block_ids.shape[0]
    return pl.pallas_call(
        functools.partial(panel_kernel, block_rows // TILE),
        out_shape=jax.ShapeDtypeStruct((count * block_rows, PANEL), jnp.float32),
        grid_spec=pltpu.PrefetchScalarGridSpec(
            num_scalar_prefetch=2,
            grid=(count,),
            in_specs=[
                pl.BlockSpec((block_rows, PANEL), lambda i, ids, _: (ids[i], 0)),
                pl.BlockSpec((children, child_rows, PANEL), lambda i, ids, _: (0, ids[i], 0)),
                whole_block((PANEL, PANEL)),
            ],
            out_specs=pl.BlockSpec((block_rows, PANEL), lambda i, ids, _: (i, 0)),
            scratch_shapes=[pltpu.VMEM((block_rows, PANEL), jnp.float32)],
        ),
        compiler_params=pltpu.CompilerParams(vmem_limit_bytes=48 * 2**20),
        name="factor_panel",
    )(block_ids, tile_map, front_panel, sent, inverse)


def two_parts(value):
    upper = value.astype(jnp.bfloat16)
    return upper, (value - upper.astype(jnp.float32)).astype(jnp.bfloat16)


def schur_kernel(rows_ref, cols_ref, parent_ref, panel_ref, *rest):
    *arrived, out_ref, split = rest
    step = pl.program_id(0)
    slab, width = out_ref.shape
    chunk = min(width, 1024)
    offset = panel_ref.shape[0] - width

    @pl.when(step == 0)
    def _():
        def cut(i, carry):
            source = pl.ds(pl.multiple_of(offset + i * SLAB, SLAB), SLAB)
            upper, lower = two_parts(panel_ref[source, :])
            target = pl.ds(pl.multiple_of(i * SLAB, SLAB), SLAB)
            split[target, 0:PANEL] = upper
            split[target, PANEL : 2 * PANEL] = lower
            split[target, 2 * PANEL : 3 * PANEL] = upper
            return carry

        lax.fori_loop(0, width // SLAB, cut, 0)

    own = panel_ref[pl.ds(pl.multiple_of(step * slab, slab), slab), :]
    upper, lower = two_parts(own)
    left = jnp.concatenate([upper, upper, lower], axis=1)
    for start in range(0, width, chunk):
        product = lax.dot_general(
            left, split[start : start + chunk, :], BY_COLUMNS, preferred_element_type=jnp.float32
        )
        out_ref[:, start : start + chunk] = parent_ref[:, start : start + chunk] - product

    slab_tiles = slab // TILE
    for index, block in enumerate(arrived):
        for r in range(block.shape[0] // TILE):
            place = rows_ref[index, r]
            local = place - step * slab_tiles

            @pl.when((place >= 0) & (local >= 0) & (local < slab_tiles))
            def _():
                rows = pl.ds(pl.multiple_of(local * TILE, TILE), TILE)
                for c in range(block.shape[1] // TILE):
                    spot = cols_ref[index, c]

                    @pl.when(spot >= 0)
                    def _():
                        columns = pl.ds(pl.multiple_of(spot * TILE, TILE), TILE)
                        out_ref[rows, columns] += block[
                            r * TILE : (r + 1) * TILE, c * TILE : (c + 1) * TILE
                        ]


def update_front(row_places, col_places, parent, panels, arrived):
    height, width = parent.shape
    slab = min(SLAB, height)

    def kept(shape):
        return pl.BlockSpec(
            shape, lambda *_: (0,) * len(shape), pipeline_mode=pl.Buffered(1)
        )

    moving = pl.BlockSpec((slab, width), lambda i, *_: (i, 0))
    return pl.pallas_call(
        schur_kernel,
        out_shape=jax.ShapeDtypeStruct((height, width), jnp.float32),
        grid_spec=pltpu.PrefetchScalarGridSpec(
            num_scalar_prefetch=2,
            grid=(height // slab,),
            in_specs=[moving, kept(panels.shape)] + [kept(block.shape) for block in arrived],
            out_specs=moving,
            scratch_shapes=[pltpu.VMEM((width, 3 * PANEL), jnp.bfloat16)],
        ),
        compiler_params=pltpu.CompilerParams(vmem_limit_bytes=56 * 2**20),
        name="update_front",
    )(row_places, col_places, parent, panels, *arrived)


def on_device(child_pivot, child_border, child_update, parent_front, tile_map):
    subs = lax.axis_size("sub")
    columns = lax.axis_size("col")
    sub_index = lax.axis_index("sub")
    row_index = lax.axis_index("row")
    column_index = lax.axis_index("col")
    group = sub_index * columns + column_index
    border = child_border[0]
    update = child_update[0]
    child_rows, half_cols = update.shape
    group_width = half_cols // subs
    parent_rows, parent_cols = parent_front.shape
    row_tiles = child_rows // TILE
    group_tiles = group_width // TILE

    pivot = lax.all_gather(child_pivot[0], "row", axis=0, tiled=True)
    all_border = lax.all_gather(border, "row", axis=0, tiled=True)
    first_columns = jnp.where(group == 0, parent_front[:, :PANEL], 0.0)
    share = lax.psum_scatter(first_columns, ("sub", "col"), scatter_dimension=0, tiled=True)
    front_panel = lax.all_gather(share, ("row", "sub", "col"), axis=0, tiled=True)

    own_map = tile_map[sub_index]
    update_parts, border_parts = [], []
    for tile in range(PANEL // TILE):
        found = own_map == tile
        live = jnp.any(found)
        at = jnp.argmax(found).astype(jnp.int32) * TILE
        part = lax.dynamic_slice_in_dim(update, at, TILE, 1)
        update_parts.append(jnp.where(live & (column_index == 0), part, 0.0))
        part = lax.dynamic_slice_in_dim(all_border, at, TILE, 0)
        border_parts.append(jnp.where(live, part, 0.0))
    picked_update = lax.psum(jnp.concatenate(update_parts, axis=1), "col")
    picked_border = jnp.concatenate(border_parts, axis=0)

    inverse = invert_pivot(pivot)
    own_factor = times_transposed(border, inverse)
    picked_factor = times_transposed(picked_border, inverse)
    picked = picked_update - times_transposed(own_factor, picked_factor)
    sent = lax.all_gather(picked, ("sub", "row"), axis=0, tiled=True)
    sent = sent.reshape(subs, -1, PANEL)

    arrived, row_places, col_places = [], [], []
    for turn in range(subs):
        piece = lax.rem(sub_index + turn, subs)
        start = piece * group_width
        far = lax.dynamic_slice_in_dim(all_border, column_index * half_cols + start, group_width, 0)
        far_factor = times_transposed(far, inverse)
        contrib = lax.dynamic_slice_in_dim(update, start, group_width, 1)
        contrib = contrib - times_transposed(own_factor, far_factor)
        moves = [
            (s * columns + c, c * subs + (s + turn) % subs)
            for s in range(subs)
            for c in range(columns)
        ]
        arrived.append(lax.ppermute(contrib, ("sub", "col"), moves))
        child = lax.rem(lax.rem(group, subs) - turn + subs, subs)
        places = tile_map[child]
        rows = lax.dynamic_slice_in_dim(places, row_index * row_tiles, row_tiles, 0)
        cols = lax.dynamic_slice_in_dim(places, group * group_tiles, group_tiles, 0)
        row_places.append(jnp.where(rows < 0, -1, rows - row_index * (parent_rows // TILE)))
        col_places.append(jnp.where(cols < 0, -1, cols - group * (parent_cols // TILE)))

    top_inverse = invert_top(tile_map, front_panel, sent, parent_rows, child_rows)
    per_group = parent_cols // parent_rows
    block_ids = jnp.concatenate(
        [row_index[None], group * per_group + jnp.arange(per_group, dtype=jnp.int32)]
    ).astype(jnp.int32)
    panels = factor_panel(
        block_ids, tile_map, front_panel, sent, top_inverse, parent_rows, child_rows
    )
    schur_block = update_front(
        jnp.stack(row_places).astype(jnp.int32),
        jnp.stack(col_places).astype(jnp.int32),
        parent_front,
        panels,
        arrived,
    )
    return (schur_block, panels[:parent_rows])


def solution(mesh):
    placed = (
        P("sub", "row", None),
        P("sub", "row", None),
        P("sub", "row", "col"),
        P("row", ("sub", "col")),
        P(),
    )
    return jax.shard_map(
        on_device,
        mesh=mesh,
        in_specs=placed,
        out_specs=(P("row", ("sub", "col")), P("row", None)),
        check_vma=False,
    )
```

```python
import functools

import jax
import jax.numpy as jnp
from jax import lax
from jax.experimental import pallas as pl
from jax.experimental.pallas import tpu as pltpu
from jax.sharding import PartitionSpec as P

PANEL = 256
TILE = 128
STRIP = 32
SLAB = 256

high = lax.Precision.HIGH
highest = lax.Precision.HIGHEST
BY_COLUMNS = (((1,), (1,)), ((), ()))


def mm(left, right):
    return jnp.dot(left, right, precision=highest, preferred_element_type=jnp.float32)


def times_transposed(left, right):
    return lax.dot_general(
        left, right, BY_COLUMNS, precision=high, preferred_element_type=jnp.float32
    )


def invert_tile(block):
    lane = lax.broadcasted_iota(jnp.int32, (STRIP, TILE), 1)
    row = lax.broadcasted_iota(jnp.int32, (STRIP, TILE), 0)
    first = 0
    rest = block
    done = []
    while first < TILE:
        strip = rest[:STRIP]
        for step in range(STRIP):
            pivot = first + step
            column = jnp.broadcast_to(strip[:, pivot : pivot + 1], (STRIP, TILE))
            scale = lax.rsqrt(column[step : step + 1])
            at_pivot = lane == pivot
            scaled = jnp.where(at_pivot[:1], 1.0, strip[step : step + 1]) * scale
            below = jnp.where(row > step, column, 0.0) * scale
            kept = jnp.where(at_pivot, 0.0, strip) - below * scaled
            strip = jnp.where(row == step, jnp.broadcast_to(scaled, (STRIP, TILE)), kept)
        done.append(strip)
        first += STRIP
        if first < TILE:
            rest = rest[STRIP:]
            columns = lax.broadcasted_iota(jnp.int32, rest.shape, 1)
            cleared = (columns >= first - STRIP) & (columns < first)
            rest = jnp.where(cleared, 0.0, rest) - mm(strip.T[first:], strip)
    whole = jnp.concatenate(done, axis=0)
    lane = lax.broadcasted_iota(jnp.int32, (TILE, TILE), 1)
    row = lax.broadcasted_iota(jnp.int32, (TILE, TILE), 0)
    return jnp.where(lane > row, 0.0, whole)


def invert_factor(work, strip):
    order = work.shape[0]
    tiles = order // TILE

    def tile_at(index):
        return pl.ds(pl.multiple_of(index * TILE, TILE), TILE)

    def eliminate(k, carry):
        here = tile_at(k)
        corner = invert_tile(work[here, here])
        strip[...] = mm(corner, work[here, :])
        strip[:, here] = corner

        def update(i, inner):
            there = tile_at(i)
            work[there, here] = jnp.zeros((TILE, TILE), jnp.float32)
            work[there, :] = work[there, :] - mm(strip[:, there].T, strip[...])
            return inner

        lax.fori_loop(k + 1, tiles, update, 0)
        columns = lax.broadcasted_iota(jnp.int32, (TILE, order), 1)
        work[here, :] = jnp.where(columns < (k + 1) * TILE, strip[...], 0.0)
        return carry

    lax.fori_loop(0, tiles, eliminate, 0)


def pivot_kernel(pivot_ref, first_ref, inverse_ref, strip):
    inverse_ref[...] = pivot_ref[...]
    invert_factor(inverse_ref, strip)


def whole_block(shape):
    return pl.BlockSpec(shape, lambda *_: (0,) * len(shape))


def invert_pivot(pivot, first):
    order = pivot.shape[0]
    return pl.pallas_call(
        pivot_kernel,
        out_shape=jax.ShapeDtypeStruct((order, order), jnp.float32),
        in_specs=[pl.BlockSpec(memory_space=pltpu.VMEM), pl.BlockSpec(memory_space=pl.ANY)],
        out_specs=pl.BlockSpec(memory_space=pltpu.VMEM),
        scratch_shapes=[pltpu.VMEM((TILE, order), jnp.float32)],
        compiler_params=pltpu.CompilerParams(vmem_limit_bytes=40 * 2**20),
        cost_estimate=pl.CostEstimate(
            flops=40 * order**3, bytes_accessed=8 * order**2, transcendentals=order
        ),
        name="invert_pivot",
    )(pivot, first)


def add_row_tiles(map_ref, first, tiles, limit, sent_ref, target):
    for child in range(sent_ref.shape[0]):
        for r in range(tiles):
            place = map_ref[child, first + r]

            @pl.when((place >= 0) & (lax.rem(jnp.maximum(place, 0), limit[0]) < limit[1]))
            def _():
                spot = lax.rem(place, limit[0])
                rows = pl.ds(pl.multiple_of(spot * TILE, TILE), TILE)
                target[rows, :] += sent_ref[child, r * TILE : (r + 1) * TILE, :]


def top_kernel(block_tiles, map_ref, front_ref, sent_ref, inverse_ref, strip):
    inverse_ref[...] = front_ref[...]
    tiles = sent_ref.shape[1] // TILE
    add_row_tiles(map_ref, 0, tiles, (block_tiles, PANEL // TILE), sent_ref, inverse_ref)
    invert_factor(inverse_ref, strip)


def invert_top(tile_map, front_panel, sent, block_rows, child_rows):
    children = sent.shape[0]
    return pl.pallas_call(
        functools.partial(top_kernel, block_rows // TILE),
        out_shape=jax.ShapeDtypeStruct((PANEL, PANEL), jnp.float32),
        grid_spec=pltpu.PrefetchScalarGridSpec(
            num_scalar_prefetch=1,
            grid=(1,),
            in_specs=[
                whole_block((PANEL, PANEL)),
                whole_block((children, child_rows, PANEL)),
            ],
            out_specs=whole_block((PANEL, PANEL)),
            scratch_shapes=[pltpu.VMEM((TILE, PANEL), jnp.float32)],
        ),
        compiler_params=pltpu.CompilerParams(vmem_limit_bytes=32 * 2**20),
        name="invert_top",
    )(tile_map, front_panel, sent)


def panel_kernel(block_tiles, ids_ref, map_ref, front_ref, sent_ref, inverse_ref, out_ref, held):
    held[...] = front_ref[...]
    tiles = sent_ref.shape[1] // TILE
    first = ids_ref[pl.program_id(0)] * tiles
    add_row_tiles(map_ref, first, tiles, (block_tiles, block_tiles), sent_ref, held)
    out_ref[...] = lax.dot_general(
        held[...], inverse_ref[...], BY_COLUMNS, precision=highest,
        preferred_element_type=jnp.float32,
    )


def factor_panel(block_ids, tile_map, front_panel, sent, inverse, block_rows, child_rows):
    children = sent.shape[0]
    count = block_ids.shape[0]
    return pl.pallas_call(
        functools.partial(panel_kernel, block_rows // TILE),
        out_shape=jax.ShapeDtypeStruct((count * block_rows, PANEL), jnp.float32),
        grid_spec=pltpu.PrefetchScalarGridSpec(
            num_scalar_prefetch=2,
            grid=(count,),
            in_specs=[
                pl.BlockSpec((block_rows, PANEL), lambda i, ids, _: (ids[i], 0)),
                pl.BlockSpec((children, child_rows, PANEL), lambda i, ids, _: (0, ids[i], 0)),
                whole_block((PANEL, PANEL)),
            ],
            out_specs=pl.BlockSpec((block_rows, PANEL), lambda i, ids, _: (i, 0)),
            scratch_shapes=[pltpu.VMEM((block_rows, PANEL), jnp.float32)],
        ),
        compiler_params=pltpu.CompilerParams(vmem_limit_bytes=48 * 2**20),
        name="factor_panel",
    )(block_ids, tile_map, front_panel, sent, inverse)


def two_parts(value):
    upper = value.astype(jnp.bfloat16)
    return upper, (value - upper.astype(jnp.float32)).astype(jnp.bfloat16)


def schur_kernel(rows_ref, cols_ref, parent_ref, panel_ref, *rest):
    *arrived, out_ref, split = rest
    step = pl.program_id(0)
    slab, width = out_ref.shape
    chunk = min(width, 1024)
    offset = panel_ref.shape[0] - width

    @pl.when(step == 0)
    def _():
        def cut(i, carry):
            source = pl.ds(pl.multiple_of(offset + i * SLAB, SLAB), SLAB)
            upper, lower = two_parts(panel_ref[source, :])
            target = pl.ds(pl.multiple_of(i * SLAB, SLAB), SLAB)
            split[target, 0:PANEL] = upper
            split[target, PANEL : 2 * PANEL] = lower
            split[target, 2 * PANEL : 3 * PANEL] = upper
            return carry

        lax.fori_loop(0, width // SLAB, cut, 0)

    own = panel_ref[pl.ds(pl.multiple_of(step * slab, slab), slab), :]
    upper, lower = two_parts(own)
    left = jnp.concatenate([upper, upper, lower], axis=1)
    for start in range(0, width, chunk):
        product = lax.dot_general(
            left, split[start : start + chunk, :], BY_COLUMNS, preferred_element_type=jnp.float32
        )
        out_ref[:, start : start + chunk] = parent_ref[:, start : start + chunk] - product

    slab_tiles = slab // TILE
    for index, block in enumerate(arrived):
        for r in range(block.shape[0] // TILE):
            place = rows_ref[index, r]
            local = place - step * slab_tiles

            @pl.when((place >= 0) & (local >= 0) & (local < slab_tiles))
            def _():
                rows = pl.ds(pl.multiple_of(local * TILE, TILE), TILE)
                for c in range(block.shape[1] // TILE):
                    spot = cols_ref[index, c]

                    @pl.when(spot >= 0)
                    def _():
                        columns = pl.ds(pl.multiple_of(spot * TILE, TILE), TILE)
                        out_ref[rows, columns] += block[
                            r * TILE : (r + 1) * TILE, c * TILE : (c + 1) * TILE
                        ]


def update_front(row_places, col_places, parent, panels, arrived):
    height, width = parent.shape
    slab = min(SLAB, height)

    def kept(shape):
        return pl.BlockSpec(
            shape, lambda *_: (0,) * len(shape), pipeline_mode=pl.Buffered(1)
        )

    moving = pl.BlockSpec((slab, width), lambda i, *_: (i, 0))
    return pl.pallas_call(
        schur_kernel,
        out_shape=jax.ShapeDtypeStruct((height, width), jnp.float32),
        grid_spec=pltpu.PrefetchScalarGridSpec(
            num_scalar_prefetch=2,
            grid=(height // slab,),
            in_specs=[moving, kept(panels.shape)] + [kept(block.shape) for block in arrived],
            out_specs=moving,
            scratch_shapes=[pltpu.VMEM((width, 3 * PANEL), jnp.bfloat16)],
        ),
        compiler_params=pltpu.CompilerParams(vmem_limit_bytes=56 * 2**20),
        name="update_front",
    )(row_places, col_places, parent, panels, *arrived)


def half_pieces(border):
    rows, columns = lax.axis_size("row"), lax.axis_size("col")
    half = rows // columns
    pieces = []
    for turn in range(half):
        moves = [
            ((half * c + (i + turn) % half) * columns + i // half, i * columns + c)
            for i in range(rows)
            for c in range(columns)
        ]
        pieces.append(lax.ppermute(border, ("row", "col"), moves))
    return pieces


def in_order(pieces, row_index):
    half = len(pieces)
    height = pieces[0].shape[0]
    result = jnp.zeros((half * height, pieces[0].shape[1]), pieces[0].dtype)
    for turn, piece in enumerate(pieces):
        place = lax.rem(row_index + turn, half) * height
        result = lax.dynamic_update_slice_in_dim(result, piece, place, 0)
    return result


def from_first(block, share, column_index):
    result = block if share is None else block[:share]
    for c in range(1, lax.axis_size("col")):
        piece = block if share is None else block[c * share : (c + 1) * share]
        result = jnp.where(column_index == c, lax.ppermute(piece, "col", [(0, c)]), result)
    return result


def on_device(child_pivot, child_border, child_update, parent_front, tile_map):
    subs = lax.axis_size("sub")
    columns = lax.axis_size("col")
    sub_index = lax.axis_index("sub")
    row_index = lax.axis_index("row")
    column_index = lax.axis_index("col")
    group = sub_index * columns + column_index
    border = child_border[0]
    update = child_update[0]
    child_rows, half_cols = update.shape
    group_width = half_cols // subs
    parent_rows, parent_cols = parent_front.shape
    row_tiles = child_rows // TILE
    group_tiles = group_width // TILE

    pivot_rows = child_pivot.shape[1] // columns
    pivot = lax.dynamic_slice_in_dim(child_pivot[0], column_index * pivot_rows, pivot_rows, 0)
    pivot = lax.all_gather(pivot, ("row", "col"), axis=0, tiled=True)
    far_border = half_pieces(border)
    first_columns = jnp.where(group == 0, parent_front[:, :PANEL], 0.0)
    share = lax.psum_scatter(first_columns, ("sub", "col"), scatter_dimension=0, tiled=True)
    front_panel = lax.all_gather(share, ("row", "sub", "col"), axis=0, tiled=True)

    own_map = tile_map[sub_index]
    split = subs * lax.axis_size("row") * child_rows * PANEL <= parent_front.size
    share_rows = child_rows // columns if split else child_rows
    share_start = column_index * share_rows if split else 0
    share_axes = ("sub", "row", "col") if split else ("sub", "row")
    update_parts, spots = [], []
    for tile in range(PANEL // TILE):
        found = own_map == tile
        live = jnp.any(found)
        at = jnp.argmax(found).astype(jnp.int32) * TILE
        part = lax.dynamic_slice_in_dim(update, at, TILE, 1)
        update_parts.append(jnp.where(live, part, 0.0))
        spots.append((live, at))
    picked_update = from_first(jnp.concatenate(update_parts, axis=1), share_rows if split else None, column_index)

    inverse = invert_pivot(pivot, share)
    far_factor = in_order([times_transposed(piece, inverse) for piece in far_border], row_index)
    own_factor = times_transposed(border, inverse)
    picked_factor = jnp.concatenate(
        [
            jnp.where(live, lax.dynamic_slice_in_dim(far_factor, at, TILE, 0), 0.0)
            for live, at in spots
        ],
        axis=0,
    )
    picked_factor = from_first(picked_factor, None, column_index)
    share_factor = lax.dynamic_slice_in_dim(own_factor, share_start, share_rows, 0)
    picked = picked_update - times_transposed(share_factor, picked_factor)
    picked = jnp.where(front_panel[0, 0] > 0.0, picked, jnp.nan)
    sent = lax.all_gather(picked, share_axes, axis=0, tiled=True)
    sent = sent.reshape(subs, -1, PANEL)

    arrived, row_places, col_places = [], [], []
    for turn in range(subs):
        piece = lax.rem(sub_index + turn, subs)
        start = piece * group_width
        far = lax.dynamic_slice_in_dim(far_factor, start, group_width, 0)
        contrib = lax.dynamic_slice_in_dim(update, start, group_width, 1)
        contrib = contrib - times_transposed(own_factor, far)
        moves = [
            (s * columns + c, c * subs + (s + turn) % subs)
            for s in range(subs)
            for c in range(columns)
        ]
        arrived.append(lax.ppermute(contrib, ("sub", "col"), moves))
        child = lax.rem(lax.rem(group, subs) - turn + subs, subs)
        places = tile_map[child]
        rows = lax.dynamic_slice_in_dim(places, row_index * row_tiles, row_tiles, 0)
        cols = lax.dynamic_slice_in_dim(places, group * group_tiles, group_tiles, 0)
        row_places.append(jnp.where(rows < 0, -1, rows - row_index * (parent_rows // TILE)))
        col_places.append(jnp.where(cols < 0, -1, cols - group * (parent_cols // TILE)))

    top_inverse = invert_top(tile_map, front_panel, sent, parent_rows, child_rows)
    per_group = parent_cols // parent_rows
    block_ids = jnp.concatenate(
        [row_index[None], group * per_group + jnp.arange(per_group, dtype=jnp.int32)]
    ).astype(jnp.int32)
    panels = factor_panel(
        block_ids, tile_map, front_panel, sent, top_inverse, parent_rows, child_rows
    )
    schur_block = update_front(
        jnp.stack(row_places).astype(jnp.int32),
        jnp.stack(col_places).astype(jnp.int32),
        parent_front,
        panels,
        arrived,
    )
    return (schur_block, panels[:parent_rows])


def solution(mesh):
    placed = (
        P("sub", "row", None),
        P("sub", "row", None),
        P("sub", "row", "col"),
        P("row", ("sub", "col")),
        P(),
    )
    return jax.shard_map(
        on_device,
        mesh=mesh,
        in_specs=placed,
        out_specs=(P("row", ("sub", "col")), P("row", None)),
        check_vma=False,
    )
```
